32 devices in a mesh: region: 2 (over core), island: 4 (over y, x), dev: 4 (over z).
Axes of the slice: x: 2, y: 2, z: 4, core: 2. Of those that a mesh axis runs over, the one named last changes fastest.
Arguments:
- activations: bfloat16 [8192, 2560], P(('region', 'island', 'dev')), may hold values from -6 to 6
- cotangent: bfloat16 [8192, 512], P(('region', 'island', 'dev')), may hold values from -6 to 6
- island_weight: float32 [2, 4, 2560, 512], P('region', 'island', 'dev'), may hold values from -6 to 6
- adam_first: float32 [2, 4, 2560, 512], P('region', 'island', 'dev'), may hold values from -6 to 6
- adam_second: float32 [2, 4, 2560, 512], P('region', 'island', 'dev'), may hold values from 0.01 to 1
- region_anchor: float32 [2, 2560, 512], P('region', 'dev'), may hold values from -6 to 6
- region_momentum: float32 [2, 2560, 512], P('region', 'dev'), may hold values from -6 to 6
- global_anchor: float32 [2560, 512], P('dev'), may hold values from -6 to 6
- global_momentum: float32 [2560, 512], P('dev'), may hold values from -6 to 6
Outputs:
- first_new: float32 [2, 4, 2560, 512], P('region', 'island', 'dev')
- second_new: float32 [2, 4, 2560, 512], P('region', 'island', 'dev')
- region_velocity: float32 [2, 2560, 512], P('region', 'dev')
- global_velocity: float32 [2560, 512], P('dev')
- global_new: float32 [2560, 512], P('dev')
- next_keys: bfloat16 [8192, 512], P(('region', 'island', 'dev'))
The draws below stay inside these ranges and needn't reach their ends.
All inputs are finite; a program needn't handle non-finite values.
Results may differ from the reference program's by a relative error of at most 0.0049.
Values may be sent and summed in bfloat16 or wider, within the bound.
No kernel may reach another device: no remote copies, remote signals or barrier semaphores. Data moves between devices by JAX's collectives and lax.ppermute only.
A program may use at most 64 MiB of HBM per device.

```python
import math
import jax
import jax.numpy as jnp
from jax import lax

DW = 2560
KV = 512
TOK_DEV = 256
TOKENS = 8192
N_REGION = 2
N_ISLAND = 4
N_DEV = 4


def raised(drawn, stream_key, source, target, blocks, factor):
    owner, partner = [(jnp.arange(drawn.shape[dim]) // (drawn.shape[dim] // blocks)).reshape([-1 if axis == dim else 1 for axis in range(drawn.ndim)]) for dim in (source, target)]
    chosen = jax.random.permutation(stream_key, blocks)[partner]
    strong = (owner == chosen) | (owner == (partner + blocks // 2) % blocks)
    return jnp.where(strong, factor * drawn, drawn)


def block_scale(rng, extent, cuts, least, largest):
    def one(axis_at, blocks):
        heights = jax.random.uniform(jax.random.fold_in(jax.random.fold_in(rng, 6), axis_at), (blocks,), jnp.float32, least / len(cuts), largest / len(cuts))
        return jnp.repeat(jnp.exp(heights), extent[axis_at] // blocks).reshape((-1,) + (1,) * (len(extent) - axis_at - 1))

    level = one(*cuts[0])
    for cut in cuts[1:]:
        level = level * one(*cut)
    return level


def normal_values(stream_key, shape, deviation, reach, pieces=(), kind=jnp.bfloat16):
    result = deviation * jax.random.normal(stream_key, shape, jnp.float32)
    if pieces:
        result = result * block_scale(stream_key, shape, pieces, -0.22, 0.18)
    return jnp.clip(result, -reach, reach).astype(kind)


def gaussian_with(key, shape, width, most, pieces, heavy, kind=jnp.bfloat16):
    array = width * jax.random.normal(key, shape, jnp.float32)
    if pieces:
        array = array * block_scale(key, shape, pieces, -0.22, 0.18)
    return jnp.clip(raised(array, jax.random.fold_in(key, 3), *heavy), -most, most).astype(kind)


def setup_inputs(seed: int = 0) -> dict:
    key_list = jax.random.split(jax.random.key(seed), 10)
    return {
        "activations": gaussian_with(key_list[0], (TOKENS, DW), 1.0, 6.0, ((0, 32),), (0, 1, 32, 2.75)),
        "cotangent": normal_values(key_list[1], (TOKENS, KV), 1.0, 6.0, ((0, 32),)),
        "island_weight": normal_values(key_list[2], (N_REGION, N_ISLAND, DW, KV), 1.0, 6.0, ((0, 2), (1, 4), (2, 4)), jnp.float32),
        "adam_first": normal_values(key_list[3], (N_REGION, N_ISLAND, DW, KV), 1.0, 6.0, ((0, 2), (1, 4), (2, 4)), jnp.float32),
        "adam_second": jnp.clip(jnp.exp(math.log(1.0) - 4.6051702 * jax.random.uniform(key_list[4], (N_REGION, N_ISLAND, DW, KV), jnp.float32) ** block_scale(key_list[4], (N_REGION, N_ISLAND, DW, KV), ((0, 2), (1, 4), (2, 4)), -0.2, 0.2)), 0.01, 1.0),
        "region_anchor": normal_values(key_list[5], (N_REGION, DW, KV), 1.0, 6.0, ((0, 2), (1, 4)), jnp.float32),
        "region_momentum": normal_values(key_list[6], (N_REGION, DW, KV), 0.5, 6.0, ((0, 2), (1, 4)), jnp.float32),
        "global_anchor": normal_values(key_list[7], (DW, KV), 1.0, 6.0, ((0, 4),), jnp.float32),
        "global_momentum": normal_values(key_list[8], (DW, KV), 0.5, 6.0, ((0, 4),), jnp.float32),
    }


beta_first = 0.9
beta_second = 0.999
adam_eps = 1e-08
inner_rate = 0.05
weight_decay = 0.1
region_mu = 0.9
region_rate = 0.7
global_mu = 0.9
global_rate = 0.7

def island_gradient(pair):
    act_part, cot_part = pair
    partials = jnp.einsum('ntd,ntk->ndk', act_part.astype(jnp.float32), cot_part.astype(jnp.float32))
    rounded = lax.optimization_barrier(partials.astype(jnp.bfloat16)).astype(jnp.float32)
    return lax.optimization_barrier(jnp.sum(rounded, axis=0))

def reference(activations, cotangent, island_weight, adam_first, adam_second, region_anchor, region_momentum, global_anchor, global_momentum):
    groups = N_REGION * N_ISLAND
    act_blocks = activations.reshape(groups, N_DEV, TOK_DEV, DW)
    cot_blocks = cotangent.reshape(groups, N_DEV, TOK_DEV, KV)
    summed = lax.map(island_gradient, (act_blocks, cot_blocks)).reshape(N_REGION, N_ISLAND, DW, KV)
    gradient = summed * (1.0 / math.sqrt(TOK_DEV * N_DEV))
    first_new = beta_first * adam_first + (1.0 - beta_first) * gradient
    second_new = beta_second * adam_second + (1.0 - beta_second) * gradient * gradient
    inner = island_weight - inner_rate * (first_new / (jnp.sqrt(second_new) + adam_eps) + weight_decay * island_weight)
    island_delta = region_anchor[:, None] - inner
    region_mean = lax.optimization_barrier(jnp.sum(island_delta, axis=1)) / N_ISLAND
    region_velocity = region_mu * region_momentum + region_mean
    region_params = region_anchor - region_rate * (region_mean + region_mu * region_velocity)
    global_mean = lax.optimization_barrier(jnp.sum(global_anchor[None] - region_params, axis=0)) / N_REGION
    global_velocity = global_mu * global_momentum + global_mean
    global_new = global_anchor - global_rate * (global_mean + global_mu * global_velocity)
    projected = jnp.dot(activations, global_new.astype(jnp.bfloat16), preferred_element_type=jnp.float32)
    next_keys = (projected * (1.0 / math.sqrt(DW))).astype(jnp.bfloat16)
    return (first_new, second_new, region_velocity, global_velocity, global_new, next_keys)
```

```python
import math

import jax
import jax.numpy as jnp
from jax import lax
from jax.sharding import PartitionSpec as P

DW = 2560
LANES = 128


beta_first = 0.9
beta_second = 0.999
adam_eps = 1e-08
inner_rate = 0.05
weight_decay = 0.1
region_mu = 0.9
region_rate = 0.7
global_mu = 0.9
global_rate = 0.7


def adam(gradient, island_weight, adam_first, adam_second):
    first_new = beta_first * adam_first + (1.0 - beta_first) * gradient
    second_new = beta_second * adam_second + (1.0 - beta_second) * gradient * gradient
    inner = island_weight - inner_rate * (
        first_new / (jnp.sqrt(second_new) + adam_eps) + weight_decay * island_weight
    )
    return first_new, second_new, inner


def regional(region_mean, region_anchor, region_momentum):
    region_velocity = region_mu * region_momentum + region_mean
    region_params = region_anchor - region_rate * (region_mean + region_mu * region_velocity)
    return region_velocity, region_params


def outer(global_mean, global_anchor, global_momentum):
    global_velocity = global_mu * global_momentum + global_mean
    global_new = global_anchor - global_rate * (global_mean + global_mu * global_velocity)
    return global_velocity, global_new


def generic_body(
    activations,
    cotangent,
    island_weight,
    adam_first,
    adam_second,
    region_anchor,
    region_momentum,
    global_anchor,
    global_momentum,
):
    island_tokens = activations.shape[0] * lax.axis_size("dev")
    islands = lax.axis_size("island")
    regions = lax.axis_size("region")
    summed = lax.psum_scatter(
        lax.dot_general(
            activations, cotangent, (((0,), (0,)), ((), ())), preferred_element_type=jnp.float32
        ).astype(jnp.bfloat16),
        "dev",
        scatter_dimension=0,
        tiled=True,
    ).astype(jnp.float32)
    gradient = summed * (1.0 / math.sqrt(island_tokens))
    first_new, second_new, inner = adam(gradient, island_weight, adam_first, adam_second)
    island_delta = region_anchor[:, None] - inner
    region_mean = lax.psum(island_delta, "island")[:, 0] / islands
    region_velocity, region_params = regional(region_mean, region_anchor, region_momentum)
    region_gap = global_anchor[None] - region_params
    global_mean = lax.psum(region_gap, "region")[0] / regions
    global_velocity, global_new = outer(global_mean, global_anchor, global_momentum)
    weight_full = lax.all_gather(global_new.astype(jnp.bfloat16), "dev", axis=0, tiled=True)
    projected = jnp.dot(activations, weight_full, preferred_element_type=jnp.float32)
    next_keys = (projected * (1.0 / math.sqrt(activations.shape[1]))).astype(jnp.bfloat16)
    return (first_new, second_new, region_velocity, global_velocity, global_new, next_keys)


def flip(array, axis, bits):
    return lax.ppermute(array, axis, [(i, i ^ bits) for i in range(lax.axis_size(axis))])


def chunks_of(rows):
    units = rows // LANES
    sizes = [1]
    while sum(sizes) < units:
        left = units - sum(sizes)
        sizes.append(2 if left >= 4 else 1)
    edges = [0]
    for size in sizes:
        edges.append(edges[-1] + size * LANES)
    return list(zip(edges[:-1], edges[1:]))


def paired_body(
    activations,
    cotangent,
    island_weight,
    adam_first,
    adam_second,
    region_anchor,
    region_momentum,
    global_anchor,
    global_momentum,
):
    devs = lax.axis_size("dev")
    islands = lax.axis_size("island")
    regions = lax.axis_size("region")
    tokens, features = activations.shape
    rows = features // devs
    scale = 1.0 / math.sqrt(tokens * devs)
    me = lax.axis_index("dev")
    low, high = me & 1, me >> 1
    core = lax.axis_index("region")
    weight, first, second = island_weight[0, 0], adam_first[0, 0], adam_second[0, 0]
    anchor, momentum = region_anchor[0], region_momentum[0]
    pieces = chunks_of(rows)

    def columns(low_bit, high_bit, start, stop):
        at = [activations[:, s * rows + start : s * rows + stop] for s in range(devs)]
        return jnp.where(
            high_bit == 0,
            jnp.where(low_bit == 0, at[0], at[1]),
            jnp.where(low_bit == 0, at[2], at[3]),
        )

    def product(left, right):
        return lax.dot_general(
            left, right, (((0,), (0,)), ((), ())), preferred_element_type=jnp.float32
        )

    other_cotangent = flip(cotangent, "dev", 1)
    arrived = []
    for start, stop in pieces:
        message = jnp.concatenate(
            [columns(1 - low, high, start, stop), columns(1 - low, 1 - high, start, stop)], axis=1
        )
        arrived.append(flip(message, "dev", 1))

    gradients, means, global_means, blocks = [], [], [], []
    for k, (start, stop) in enumerate(pieces):
        size = stop - start
        raw = arrived[k]
        away = product(columns(low, 1 - high, start, stop), cotangent) + product(
            raw[:, size:], other_cotangent
        )
        kept = product(columns(low, high, start, stop), cotangent) + product(
            raw[:, :size], other_cotangent
        )
        summed = kept + flip(away.astype(jnp.bfloat16), "dev", 2).astype(jnp.float32)
        gradient = summed * scale
        gradients.append(gradient)
        _, _, inner = adam(gradient, weight[start:stop], first[start:stop], second[start:stop])
        total = (anchor[start:stop] - inner).astype(jnp.bfloat16)
        order = [1, 2] if k % 2 == 0 else [2, 1]
        for i, bits in enumerate(order):
            total = total.astype(jnp.float32) + flip(total, "island", bits).astype(jnp.float32)
            if i < len(order) - 1:
                total = total.astype(jnp.bfloat16)
        region_mean = total / islands
        means.append(region_mean)
        _, region_params = regional(region_mean, anchor[start:stop], momentum[start:stop])
        gap = global_anchor[start:stop] - region_params
        global_mean = (gap + flip(gap, "region", 1)) / regions
        global_means.append(global_mean)
        _, fresh = outer(global_mean, global_anchor[start:stop], global_momentum[start:stop])
        low_weight = fresh.astype(jnp.bfloat16)
        half = size // 2
        mine = jnp.where(core == 0, low_weight[:half], low_weight[half:])
        held = jnp.stack([mine] + [flip(mine, "dev", bits) for bits in range(1, devs)])
        swapped = flip(held, "region", 1)
        blocks.append((held, swapped))

    projected = jnp.zeros((tokens, cotangent.shape[1]), jnp.float32)
    for (start, stop), (held, swapped) in zip(pieces, blocks):
        half = (stop - start) // 2
        for bits in range(devs):
            left = columns(low ^ (bits & 1), high ^ (bits >> 1), start, stop)
            upper = jnp.where(core == 0, held[bits], swapped[bits])
            lower = jnp.where(core == 0, swapped[bits], held[bits])
            projected += jnp.dot(left[:, :half], upper, preferred_element_type=jnp.float32)
            projected += jnp.dot(left[:, half:], lower, preferred_element_type=jnp.float32)
    next_keys = (projected * (1.0 / math.sqrt(features))).astype(jnp.bfloat16)

    first_new, second_new, _ = adam(jnp.concatenate(gradients), weight, first, second)
    region_velocity, _ = regional(jnp.concatenate(means), anchor, momentum)
    global_velocity, global_new = outer(
        jnp.concatenate(global_means), global_anchor, global_momentum
    )
    return (
        first_new[None, None],
        second_new[None, None],
        region_velocity[None],
        global_velocity,
        global_new,
        next_keys,
    )


def solution(mesh):
    devs, islands, regions = mesh.shape["dev"], mesh.shape["island"], mesh.shape["region"]
    aligned = DW % (devs * LANES) == 0
    paired = devs == 4 and islands == 4 and regions == 2 and aligned
    return jax.shard_map(
        paired_body if paired else generic_body,
        mesh=mesh,
        in_specs=(
            P(("region", "island", "dev"), None),
            P(("region", "island", "dev"), None),
            P("region", "island", "dev", None),
            P("region", "island", "dev", None),
            P("region", "island", "dev", None),
            P("region", "dev", None),
            P("region", "dev", None),
            P("dev", None),
            P("dev", None),
        ),
        out_specs=(
            P("region", "island", "dev", None),
            P("region", "island", "dev", None),
            P("region", "dev", None),
            P("dev", None),
            P("dev", None),
            P(("region", "island", "dev"), None),
        ),
        check_vma=False,
    )
```

```python
import math

import jax
import jax.numpy as jnp
from jax import lax
from jax.experimental import pallas as pl
from jax.experimental.pallas import tpu as pltpu
from jax.sharding import PartitionSpec as P

DW = 2560
LANES = 128
VMEM_BYTES = 16 * 2**20
SIZES = [2, 3]
GROUPS = [[0], [1]]
SHARE = 3
ORDER = ("c0", "c1", "x0", "x1", "b0", "s0", "s1", "a0", "p0", "q0", "a1", "p1", "m1", "k0", "j0", "q1", "v1", "o1", "k1", "j1")


beta_first = 0.9
beta_second = 0.999
adam_eps = 1e-08
inner_rate = 0.05
weight_decay = 0.1
region_mu = 0.9
region_rate = 0.7
global_mu = 0.9
global_rate = 0.7


def moments(gradient, adam_first, adam_second):
    first_new = beta_first * adam_first + (1.0 - beta_first) * gradient
    second_new = beta_second * adam_second + (1.0 - beta_second) * gradient * gradient
    return first_new, second_new


def adam(gradient, island_weight, adam_first, adam_second):
    first_new, second_new = moments(gradient, adam_first, adam_second)
    inner = island_weight - inner_rate * (
        first_new / (jnp.sqrt(second_new) + adam_eps) + weight_decay * island_weight
    )
    return first_new, second_new, inner


def regional(region_mean, region_anchor, region_momentum):
    region_velocity = region_mu * region_momentum + region_mean
    region_params = region_anchor - region_rate * (region_mean + region_mu * region_velocity)
    return region_velocity, region_params


def outer(global_mean, global_anchor, global_momentum):
    global_velocity = global_mu * global_momentum + global_mean
    global_new = global_anchor - global_rate * (global_mean + global_mu * global_velocity)
    return global_velocity, global_new


def generic_body(
    activations,
    cotangent,
    island_weight,
    adam_first,
    adam_second,
    region_anchor,
    region_momentum,
    global_anchor,
    global_momentum,
):
    island_tokens = activations.shape[0] * lax.axis_size("dev")
    islands = lax.axis_size("island")
    regions = lax.axis_size("region")
    summed = lax.psum_scatter(
        lax.dot_general(
            activations, cotangent, (((0,), (0,)), ((), ())), preferred_element_type=jnp.float32
        ).astype(jnp.bfloat16),
        "dev",
        scatter_dimension=0,
        tiled=True,
    ).astype(jnp.float32)
    gradient = summed * (1.0 / math.sqrt(island_tokens))
    first_new, second_new, inner = adam(gradient, island_weight, adam_first, adam_second)
    island_delta = region_anchor[:, None] - inner
    region_mean = lax.psum(island_delta, "island")[:, 0] / islands
    region_velocity, region_params = regional(region_mean, region_anchor, region_momentum)
    region_gap = global_anchor[None] - region_params
    global_mean = lax.psum(region_gap, "region")[0] / regions
    global_velocity, global_new = outer(global_mean, global_anchor, global_momentum)
    weight_full = lax.all_gather(global_new.astype(jnp.bfloat16), "dev", axis=0, tiled=True)
    projected = jnp.dot(activations, weight_full, preferred_element_type=jnp.float32)
    next_keys = (projected * (1.0 / math.sqrt(activations.shape[1]))).astype(jnp.bfloat16)
    return (first_new, second_new, region_velocity, global_velocity, global_new, next_keys)


def flip(array, axis, bits):
    return lax.ppermute(array, axis, [(i, i ^ bits) for i in range(lax.axis_size(axis))])


def chunks_of(rows):
    units = rows // LANES
    sizes = SIZES if sum(SIZES) == units else [1] * units
    edges = [0]
    for size in sizes:
        edges.append(edges[-1] + size * LANES)
    return list(zip(edges[:-1], edges[1:]))


def local_kernel(kernel, out_shapes, place, *operands, order):
    def with_order(place_ref, *refs):
        kernel(place_ref, *refs[len(order) :])

    whole = pl.BlockSpec(memory_space=pltpu.VMEM)
    return pl.pallas_call(
        with_order,
        out_shape=[jax.ShapeDtypeStruct(shape, dtype) for shape, dtype in out_shapes],
        in_specs=[pl.BlockSpec(memory_space=pltpu.SMEM)]
        + [pl.BlockSpec(memory_space=pl.ANY)] * len(order)
        + [whole] * len(operands),
        out_specs=[whole] * len(out_shapes),
        compiler_params=pltpu.CompilerParams(vmem_limit_bytes=VMEM_BYTES),
        cost_estimate=pl.CostEstimate(flops=1, bytes_accessed=1, transcendentals=0),
    )(place, *order, *operands)


def flipped(place, bits):
    return 2 * (place[1] ^ (bits >> 1)) + (place[0] ^ (bits & 1))


def product(left, right):
    return lax.dot_general(
        left, right, (((0,), (0,)), ((), ())), preferred_element_type=jnp.float32
    )


def paired_body(
    activations,
    cotangent,
    island_weight,
    adam_first,
    adam_second,
    region_anchor,
    region_momentum,
    global_anchor,
    global_momentum,
):
    f32, bf16 = jnp.float32, jnp.bfloat16
    devs = lax.axis_size("dev")
    islands = lax.axis_size("island")
    regions = lax.axis_size("region")
    tokens, features = activations.shape
    width = cotangent.shape[1]
    half = width // regions
    rows = features // devs
    scale = 1.0 / math.sqrt(tokens * devs)
    me = lax.axis_index("dev")
    place = jnp.stack([me & 1, me >> 1, lax.axis_index("region")]).astype(jnp.int32)
    weight, first, second = island_weight[0, 0], adam_first[0, 0], adam_second[0, 0]
    anchor, momentum = region_anchor[0], region_momentum[0]
    pieces = chunks_of(rows)
    groups = groups_of(len(pieces))
    spans = [(pieces[members[0]][0], pieces[members[-1]][1]) for members in groups]
    group = [{} for _ in groups]
    bases = []
    token = [place]
    state = [{} for _ in pieces]

    def run(kernel, out_shapes, *operands, late=None):
        order = [token[0]]
        if late is not None:
            order.append(group[late]["held"][0])
        outs = local_kernel(kernel, out_shapes, place, *operands, order=order)
        token[0] = outs[0]
        return outs

    def columns(shard, start, size):
        return pl.ds(pl.multiple_of(shard * rows + start, LANES), size)

    def stage_message(k):
        start, stop = pieces[k]
        size = stop - start
        extra = width if k == 0 else 0

        def kernel(place_ref, *refs):
            a_ref, out_ref = refs[0], refs[-1]
            for i, bits in enumerate((1, 3)):
                at = columns(flipped(place_ref, bits), start, size)
                out_ref[:, i * size : (i + 1) * size] = a_ref[:, at]
            if extra:
                out_ref[:, 2 * size :] = refs[1][...]

        operands = (activations, cotangent) if extra else (activations,)
        (message,) = run(kernel, [((tokens, 2 * size + extra), bf16)], *operands)
        state[k]["raw"] = flip(message, "dev", 1)

    def stage_own(k):
        start, stop = pieces[k]
        size = stop - start

        def kernel(place_ref, a_ref, c_ref, kept_ref, away_ref):
            for bits, ref in ((0, kept_ref), (2, away_ref)):
                at = columns(flipped(place_ref, bits), start, size)
                ref[...] = product(a_ref[:, at], c_ref[...])

        state[k]["own"] = run(kernel, [((size, width), f32)] * 2, activations, cotangent)

    def partner_cotangent(first_ref):
        return first_ref[:, first_ref.shape[1] - width :]

    def stage_sums(k):
        start, stop = pieces[k]
        size = stop - start

        def kernel(place_ref, own_ref, raw_ref, *refs):
            first_ref = refs[0] if k else raw_ref
            out_ref = refs[-1]
            part = product(raw_ref[:, size : 2 * size], partner_cotangent(first_ref))
            out_ref[...] = (own_ref[...] + part).astype(bf16)

        operands = [state[k]["own"][1], state[k]["raw"]] + ([state[0]["raw"]] if k else [])
        (sums,) = run(kernel, [((size, width), bf16)], *operands)
        state[k]["sum"] = flip(sums, "dev", 2)

    def stage_bases(k):
        def kernel(place_ref, w_ref, r_ref, rm_ref, g_ref, gm_ref, delta_ref, gap_ref, new_ref):
            delta_ref[...] = r_ref[...] - (1.0 - inner_rate * weight_decay) * w_ref[...]
            _, params = regional(0.0, r_ref[...], rm_ref[...])
            gap_ref[...] = g_ref[...] - params
            _, new_ref[...] = outer(0.0, g_ref[...], gm_ref[...])

        bases[:] = run(
            kernel,
            [((rows, width), f32)] * 3,
            weight,
            anchor,
            momentum,
            global_anchor,
            global_momentum,
        )
        bases.append(flip(bases[1], "region", 1))

    def stage_adam(g):
        members = groups[g]
        start, stop = spans[g]
        size = stop - start

        def kernel(place_ref, m_ref, v_ref, base_ref, first_ref, *refs):
            delta_ref, gradient_ref = refs[-2:]
            for i, k in enumerate(members):
                low, high = pieces[k]
                count = high - low
                own_ref, raw_ref, sum_ref = refs[3 * i : 3 * i + 3]
                part = product(raw_ref[:, :count], partner_cotangent(first_ref))
                gradient = (own_ref[...] + part + sum_ref[...].astype(f32)) * scale
                span = pl.ds(low, count)
                first_new, second_new = moments(gradient, m_ref[span, :], v_ref[span, :])
                step = inner_rate * (first_new / (jnp.sqrt(second_new) + adam_eps))
                here = pl.ds(low - start, count)
                delta_ref[here, :] = (base_ref[span, :] + step).astype(bf16)
                gradient_ref[here, :] = gradient

        operands = [first, second, bases[0], state[0]["raw"]]
        for k in members:
            operands += [state[k]["own"][0], state[k]["raw"], state[k]["sum"]]
        delta, gradient = run(kernel, [((size, width), bf16), ((size, width), f32)], *operands)
        group[g].update(delta=delta, gradient=gradient, pair=halves(delta, (1, 2)))

    def halves(array, bits):
        middle = array.shape[0] // 2
        return [flip(array[:middle], "island", bits[0]), flip(array[middle:], "island", bits[1])]

    def summed(mine_ref, upper_ref, lower_ref):
        other = jnp.concatenate([upper_ref[...], lower_ref[...]], axis=0)
        return mine_ref[...].astype(f32) + other.astype(f32)

    def stage_pair(k):
        def kernel(place_ref, mine_ref, upper_ref, lower_ref, out_ref):
            out_ref[...] = summed(mine_ref, upper_ref, lower_ref).astype(bf16)

        (pair,) = run(
            kernel, [(group[k]["delta"].shape, bf16)], group[k]["delta"], *group[k]["pair"]
        )
        rest = halves(pair, (2, 1))
        group[k].update(mine=pair, rest=rest, mine2=flip(pair, "region", 1))
        group[k]["rest2"] = [flip(part, "region", 1) for part in rest]

    def stage_means(k):
        start, stop = spans[k]
        size = stop - start
        span = pl.ds(start, size)

        def kernel(place_ref, mine, up, low, mine2, up2, low2, base, base2, new, *outs):
            fresh_ref, share_ref, mean_ref, global_ref = outs
            gain = region_rate * (1.0 + region_mu)
            mean = summed(mine, up, low) / islands
            mean_ref[...] = mean
            gap = base[span, :] + gain * mean
            gap += base2[span, :] + gain * (summed(mine2, up2, low2) / islands)
            mean = gap / regions
            global_ref[...] = mean
            fresh = new[span, :] - global_rate * (1.0 + global_mu) * mean
            fresh_ref[...] = fresh.astype(bf16)
            at = pl.ds(pl.multiple_of(place_ref[2] * half, LANES), half)
            share_ref[...] = fresh_ref[:, at]

        this = group[k]
        fresh, share, mean, global_mean = run(
            kernel,
            [((size, width), bf16), ((size, half), bf16)] + [((size, width), f32)] * 2,
            this["mine"],
            *this["rest"],
            this["mine2"],
            *this["rest2"],
            bases[1],
            bases[3],
            bases[2],
        )
        held = [flip(share, "dev", bits) for bits in range(1, devs)]
        this.update(mean=mean, fresh=fresh, share=share, global_mean=global_mean, held=held)

    def left_columns(place_ref, a_ref, k):
        start, stop = spans[k]
        return [
            a_ref[:, columns(flipped(place_ref, bits), start, stop - start)]
            for bits in range(devs)
        ]

    def cuts_of(k):
        size = spans[k][1] - spans[k][0]
        cut = size * SHARE // 4
        return [(0, size)] if k == len(groups) - 1 else [(0, cut), (cut, size)]

    def stage_near(k):
        size = spans[k][1] - spans[k][0]
        cuts = cuts_of(k)

        def kernel(place_ref, a_ref, share_ref, *refs):
            held, outs, near_ref = refs[: devs - 1], refs[devs - 1 : -1], refs[-1]
            left = left_columns(place_ref, a_ref, k)
            for stack_ref, (low, high) in zip(outs, cuts):
                for i in range(devs - 1):
                    stack_ref[i] = held[i][low:high, :]
            value = jnp.dot(left[0], share_ref[...], preferred_element_type=f32)
            for bits in range(1, devs):
                value += jnp.dot(left[bits], held[bits - 1][...], preferred_element_type=f32)
            near_ref[...] = value

        *stacks, near = run(
            kernel,
            [((devs - 1, high - low, half), bf16) for low, high in cuts]
            + [((tokens, half), f32)],
            activations,
            group[k]["share"],
            *group[k]["held"],
        )
        group[k].update(near=near, swapped=[flip(stack, "region", 1) for stack in stacks])

    def stage_project(k):
        final = k == len(groups) - 1
        cuts = cuts_of(k)

        def kernel(place_ref, a_ref, fresh_ref, near_ref, *refs):
            swapped, out_ref = refs[: len(cuts)], refs[-1]
            left = left_columns(place_ref, a_ref, k)
            core = place_ref[2]
            near_at = pl.ds(pl.multiple_of(core * half, LANES), half)
            far_at = pl.ds(pl.multiple_of((1 - core) * half, LANES), half)
            far = jnp.dot(left[0], fresh_ref[:, far_at], preferred_element_type=f32)
            for bits in range(1, devs):
                right = [part[bits - 1] for part in swapped]
                right = jnp.concatenate(right, axis=0) if len(right) > 1 else right[0]
                far += jnp.dot(left[bits], right, preferred_element_type=f32)
            for value, at in ((near_ref[...], near_at), (far, far_at)):
                if k:
                    value = value + refs[len(cuts)][:, at]
                if final:
                    value = value * (1.0 / math.sqrt(features))
                out_ref[:, at] = value.astype(out_ref.dtype)

        operands = [activations, group[k]["fresh"], group[k]["near"], *group[k]["swapped"]]
        operands += [group[k - 1]["total"]] if k else []
        (total,) = run(kernel, [((tokens, width), bf16 if final else f32)], *operands)
        group[k]["total"] = total

    results = {}

    def stage_moments(k):
        def kernel(place_ref, m_ref, v_ref, *refs):
            for part, span in zip(refs, [pl.ds(low, high - low) for low, high in spans]):
                refs[-2][span, :], refs[-1][span, :] = moments(
                    part[...], m_ref[span, :], v_ref[span, :]
                )

        results["moments"] = run(
            kernel,
            [((rows, width), f32)] * 2,
            first,
            second,
            *[p["gradient"] for p in group],
            late=0,
        )

    def stage_velocity(k):
        def kernel(place_ref, m_ref, *refs):
            for part, span in zip(refs, [pl.ds(low, high - low) for low, high in spans]):
                refs[-1][span, :] = region_mu * m_ref[span, :] + part[...]

        results["velocity"] = run(
            kernel, [((rows, width), f32)], momentum, *[p["mean"] for p in group], late=-1
        )

    def stage_outer(k):
        def kernel(place_ref, g_ref, m_ref, *refs):
            for part, span in zip(refs, [pl.ds(low, high - low) for low, high in spans]):
                velocity, fresh = outer(part[...], g_ref[span, :], m_ref[span, :])
                refs[-2][span, :] = velocity
                refs[-1][span, :] = fresh

        results["outer"] = run(
            kernel,
            [((rows, width), f32)] * 2,
            global_anchor,
            global_momentum,
            *[p["global_mean"] for p in group],
        )

    stages = {
        "c": stage_message,
        "x": stage_own,
        "s": stage_sums,
        "b": stage_bases,
        "a": stage_adam,
        "p": stage_pair,
        "q": stage_means,
        "k": stage_near,
        "j": stage_project,
        "m": stage_moments,
        "v": stage_velocity,
        "o": stage_outer,
    }
    for step in plan_of(len(pieces), len(groups)):
        stages[step[0]](int(step[1:]))

    return (
        results["moments"][0][None, None],
        results["moments"][1][None, None],
        results["velocity"][0][None],
        results["outer"][0],
        results["outer"][1],
        group[-1]["total"],
    )


def groups_of(count):
    return GROUPS if count == len(SIZES) else [[k] for k in range(count)]


def plan_of(count, groups):
    if count == len(SIZES):
        return ORDER
    steps = ["c%d" % k for k in range(count)] + ["x%d" % k for k in range(count)]
    steps += ["s%d" % k for k in range(count)] + ["b0"]
    for letter in "apqkj":
        steps += [letter + "%d" % k for k in range(groups)]
    return steps + ["m0", "v0", "o0"]


def solution(mesh):
    devs, islands, regions = mesh.shape["dev"], mesh.shape["island"], mesh.shape["region"]
    aligned = DW % (devs * LANES) == 0
    paired = devs == 4 and islands == 4 and regions == 2 and aligned
    return jax.shard_map(
        paired_body if paired else generic_body,
        mesh=mesh,
        in_specs=(
            P(("region", "island", "dev"), None),
            P(("region", "island", "dev"), None),
            P("region", "island", "dev", None),
            P("region", "island", "dev", None),
            P("region", "island", "dev", None),
            P("region", "dev", None),
            P("region", "dev", None),
            P("dev", None),
            P("dev", None),
        ),
        out_specs=(
            P("region", "island", "dev", None),
            P("region", "island", "dev", None),
            P("region", "dev", None),
            P("dev", None),
            P("dev", None),
            P(("region", "island", "dev"), None),
        ),
        check_vma=False,
    )
```

```python
import math

import jax
import jax.numpy as jnp
from jax import lax
from jax.experimental import pallas as pl
from jax.experimental.pallas import tpu as pltpu
from jax.sharding import PartitionSpec as P

DW = 2560
LANES = 128
VMEM_BYTES = 16 * 2**20
SIZES = [2, 3]
GROUPS = [[0], [1]]
SHARES = (3 / 4, 1.0)
ORDER = ("c0", "c1", "x0", "x1", "b0", "s0", "s1", "a0", "p0", "q0", "a1", "p1", "k0", "j0", "q1", "v1", "y1", "o1", "m1", "k1", "j1")


beta_first = 0.9
beta_second = 0.999
adam_eps = 1e-08
inner_rate = 0.05
weight_decay = 0.1
region_mu = 0.9
region_rate = 0.7
global_mu = 0.9
global_rate = 0.7


def moments(gradient, adam_first, adam_second):
    first_new = beta_first * adam_first + (1.0 - beta_first) * gradient
    second_new = beta_second * adam_second + (1.0 - beta_second) * gradient * gradient
    return first_new, second_new


def adam(gradient, island_weight, adam_first, adam_second):
    first_new, second_new = moments(gradient, adam_first, adam_second)
    inner = island_weight - inner_rate * (
        first_new / (jnp.sqrt(second_new) + adam_eps) + weight_decay * island_weight
    )
    return first_new, second_new, inner


def regional(region_mean, region_anchor, region_momentum):
    region_velocity = region_mu * region_momentum + region_mean
    region_params = region_anchor - region_rate * (region_mean + region_mu * region_velocity)
    return region_velocity, region_params


def outer(global_mean, global_anchor, global_momentum):
    global_velocity = global_mu * global_momentum + global_mean
    global_new = global_anchor - global_rate * (global_mean + global_mu * global_velocity)
    return global_velocity, global_new


def generic_body(
    activations,
    cotangent,
    island_weight,
    adam_first,
    adam_second,
    region_anchor,
    region_momentum,
    global_anchor,
    global_momentum,
):
    island_tokens = activations.shape[0] * lax.axis_size("dev")
    islands = lax.axis_size("island")
    regions = lax.axis_size("region")
    summed = lax.psum_scatter(
        lax.dot_general(
            activations, cotangent, (((0,), (0,)), ((), ())), preferred_element_type=jnp.float32
        ).astype(jnp.bfloat16),
        "dev",
        scatter_dimension=0,
        tiled=True,
    ).astype(jnp.float32)
    gradient = summed * (1.0 / math.sqrt(island_tokens))
    first_new, second_new, inner = adam(gradient, island_weight, adam_first, adam_second)
    island_delta = region_anchor[:, None] - inner
    region_mean = lax.psum(island_delta, "island")[:, 0] / islands
    region_velocity, region_params = regional(region_mean, region_anchor, region_momentum)
    region_gap = global_anchor[None] - region_params
    global_mean = lax.psum(region_gap, "region")[0] / regions
    global_velocity, global_new = outer(global_mean, global_anchor, global_momentum)
    weight_full = lax.all_gather(global_new.astype(jnp.bfloat16), "dev", axis=0, tiled=True)
    projected = jnp.dot(activations, weight_full, preferred_element_type=jnp.float32)
    next_keys = (projected * (1.0 / math.sqrt(activations.shape[1]))).astype(jnp.bfloat16)
    return (first_new, second_new, region_velocity, global_velocity, global_new, next_keys)


def flip(array, axis, bits):
    return lax.ppermute(array, axis, [(i, i ^ bits) for i in range(lax.axis_size(axis))])


def chunks_of(rows):
    units = rows // LANES
    sizes = SIZES if sum(SIZES) == units else [1] * units
    edges = [0]
    for size in sizes:
        edges.append(edges[-1] + size * LANES)
    return list(zip(edges[:-1], edges[1:]))


def local_kernel(kernel, out_shapes, place, *operands, order):
    def with_order(place_ref, *refs):
        kernel(place_ref, *refs[len(order) :])

    whole = pl.BlockSpec(memory_space=pltpu.VMEM)
    return pl.pallas_call(
        with_order,
        out_shape=[jax.ShapeDtypeStruct(shape, dtype) for shape, dtype in out_shapes],
        in_specs=[pl.BlockSpec(memory_space=pltpu.SMEM)]
        + [pl.BlockSpec(memory_space=pl.ANY)] * len(order)
        + [whole] * len(operands),
        out_specs=[whole] * len(out_shapes),
        compiler_params=pltpu.CompilerParams(vmem_limit_bytes=VMEM_BYTES),
        cost_estimate=pl.CostEstimate(flops=1, bytes_accessed=1, transcendentals=0),
    )(place, *order, *operands)


def flipped(place, bits):
    return 2 * (place[1] ^ (bits >> 1)) + (place[0] ^ (bits & 1))


def product(left, right):
    return lax.dot_general(
        left, right, (((0,), (0,)), ((), ())), preferred_element_type=jnp.float32
    )


def paired_body(
    activations,
    cotangent,
    island_weight,
    adam_first,
    adam_second,
    region_anchor,
    region_momentum,
    global_anchor,
    global_momentum,
):
    f32, bf16 = jnp.float32, jnp.bfloat16
    devs = lax.axis_size("dev")
    islands = lax.axis_size("island")
    regions = lax.axis_size("region")
    tokens, features = activations.shape
    width = cotangent.shape[1]
    half = width // regions
    rows = features // devs
    scale = 1.0 / math.sqrt(tokens * devs)
    me = lax.axis_index("dev")
    place = jnp.stack([me & 1, me >> 1, lax.axis_index("region")]).astype(jnp.int32)
    weight, first, second = island_weight[0, 0], adam_first[0, 0], adam_second[0, 0]
    anchor, momentum = region_anchor[0], region_momentum[0]
    pieces = chunks_of(rows)
    groups = groups_of(len(pieces))
    spans = [(pieces[members[0]][0], pieces[members[-1]][1]) for members in groups]
    group = [{} for _ in groups]
    bases = []
    token = [place]
    state = [{} for _ in pieces]

    def run(kernel, out_shapes, *operands, late=None, mark=False):
        order = [token[0]]
        if late is not None:
            order.append(group[late]["held"][0])
        if mark:

            def marked(place_ref, *refs):
                kernel(place_ref, *refs[:-1])
                refs[-1][...] = jnp.zeros_like(refs[-1])

            small = (8, LANES)
            *outs, token[0] = local_kernel(
                marked, [*out_shapes, (small, f32)], place, *operands, order=order
            )
            return outs
        outs = local_kernel(kernel, out_shapes, place, *operands, order=order)
        token[0] = outs[0]
        return outs

    def columns(shard, start, size):
        return pl.ds(pl.multiple_of(shard * rows + start, LANES), size)

    def stage_message(k):
        start, stop = pieces[k]
        size = stop - start
        extra = width if k == 0 else 0

        def kernel(place_ref, *refs):
            a_ref, out_ref = refs[0], refs[-1]
            for i, bits in enumerate((1, 3)):
                at = columns(flipped(place_ref, bits), start, size)
                out_ref[:, i * size : (i + 1) * size] = a_ref[:, at]
            if extra:
                out_ref[:, 2 * size :] = refs[1][...]

        operands = (activations, cotangent) if extra else (activations,)
        (message,) = run(kernel, [((tokens, 2 * size + extra), bf16)], *operands)
        state[k]["raw"] = flip(message, "dev", 1)

    def stage_own(k):
        start, stop = pieces[k]
        size = stop - start

        def kernel(place_ref, a_ref, c_ref, kept_ref, away_ref):
            for bits, ref in ((0, kept_ref), (2, away_ref)):
                at = columns(flipped(place_ref, bits), start, size)
                ref[...] = product(a_ref[:, at], c_ref[...])

        state[k]["own"] = run(kernel, [((size, width), f32)] * 2, activations, cotangent)

    def partner_cotangent(first_ref):
        return first_ref[:, first_ref.shape[1] - width :]

    def stage_sums(k):
        start, stop = pieces[k]
        size = stop - start

        def kernel(place_ref, own_ref, raw_ref, *refs):
            first_ref = refs[0] if k else raw_ref
            out_ref = refs[-1]
            part = product(raw_ref[:, size : 2 * size], partner_cotangent(first_ref))
            out_ref[...] = (own_ref[...] + part).astype(bf16)

        operands = [state[k]["own"][1], state[k]["raw"]] + ([state[0]["raw"]] if k else [])
        (sums,) = run(kernel, [((size, width), bf16)], *operands)
        state[k]["sum"] = flip(sums, "dev", 2)

    def stage_bases(k):
        def kernel(place_ref, w_ref, r_ref, rm_ref, g_ref, gm_ref, delta_ref, gap_ref, new_ref):
            delta_ref[...] = r_ref[...] - (1.0 - inner_rate * weight_decay) * w_ref[...]
            _, params = regional(0.0, r_ref[...], rm_ref[...])
            gap_ref[...] = g_ref[...] - params
            _, new_ref[...] = outer(0.0, g_ref[...], gm_ref[...])

        bases[:] = run(
            kernel,
            [((rows, width), f32)] * 3,
            weight,
            anchor,
            momentum,
            global_anchor,
            global_momentum,
        )
        bases.append(flip(bases[1], "region", 1))

    def stage_adam(g):
        members = groups[g]
        start, stop = spans[g]
        size = stop - start

        def kernel(place_ref, m_ref, v_ref, base_ref, first_ref, *refs):
            delta_ref, gradient_ref = refs[-2:]
            for i, k in enumerate(members):
                low, high = pieces[k]
                count = high - low
                own_ref, raw_ref, sum_ref = refs[3 * i : 3 * i + 3]
                part = product(raw_ref[:, :count], partner_cotangent(first_ref))
                gradient = (own_ref[...] + part + sum_ref[...].astype(f32)) * scale
                span = pl.ds(low, count)
                first_new, second_new = moments(gradient, m_ref[span, :], v_ref[span, :])
                step = inner_rate * (first_new / (jnp.sqrt(second_new) + adam_eps))
                here = pl.ds(low - start, count)
                delta_ref[here, :] = (base_ref[span, :] + step).astype(bf16)
                gradient_ref[here, :] = gradient

        operands = [first, second, bases[0], state[0]["raw"]]
        for k in members:
            operands += [state[k]["own"][0], state[k]["raw"], state[k]["sum"]]
        delta, gradient = run(kernel, [((size, width), bf16), ((size, width), f32)], *operands)
        group[g].update(delta=delta, gradient=gradient, pair=halves(delta, (1, 2)))

    def halves(array, bits):
        middle = array.shape[0] // 2
        return [flip(array[:middle], "island", bits[0]), flip(array[middle:], "island", bits[1])]

    def summed(mine_ref, upper_ref, lower_ref):
        other = jnp.concatenate([upper_ref[...], lower_ref[...]], axis=0)
        return mine_ref[...].astype(f32) + other.astype(f32)

    def stage_pair(k):
        def kernel(place_ref, mine_ref, upper_ref, lower_ref, out_ref):
            out_ref[...] = summed(mine_ref, upper_ref, lower_ref).astype(bf16)

        (pair,) = run(
            kernel, [(group[k]["delta"].shape, bf16)], group[k]["delta"], *group[k]["pair"]
        )
        rest = halves(pair, (2, 1))
        group[k].update(mine=pair, rest=rest, mine2=flip(pair, "region", 1))
        group[k]["rest2"] = [flip(part, "region", 1) for part in rest]

    def stage_means(k):
        start, stop = spans[k]
        size = stop - start
        span = pl.ds(start, size)

        def kernel(place_ref, mine, up, low, mine2, up2, low2, base, base2, new, *outs):
            fresh_ref, share_ref, mean_ref, global_ref = outs
            gain = region_rate * (1.0 + region_mu)
            mean = summed(mine, up, low) / islands
            mean_ref[...] = mean
            gap = base[span, :] + gain * mean
            gap += base2[span, :] + gain * (summed(mine2, up2, low2) / islands)
            mean = gap / regions
            global_ref[...] = mean
            fresh = new[span, :] - global_rate * (1.0 + global_mu) * mean
            fresh_ref[...] = fresh.astype(bf16)
            at = pl.ds(pl.multiple_of(place_ref[2] * half, LANES), half)
            share_ref[...] = fresh_ref[:, at]

        this = group[k]
        fresh, share, mean, global_mean = run(
            kernel,
            [((size, width), bf16), ((size, half), bf16)] + [((size, width), f32)] * 2,
            this["mine"],
            *this["rest"],
            this["mine2"],
            *this["rest2"],
            bases[1],
            bases[3],
            bases[2],
        )
        held = [flip(share, "dev", 1), flip(share, "dev", 2)]
        if k < len(groups) - 1:
            held.append(flip(share, "dev", 3))
        this.update(mean=mean, fresh=fresh, share=share, global_mean=global_mean, held=held)

    def stage_relay(k):
        def kernel(place_ref, block_ref, out_ref):
            out_ref[...] = block_ref[...]

        block = group[k]["held"][1]
        (block,) = run(kernel, [(block.shape, bf16)], block)
        group[k]["held"].append(flip(block, "dev", 1))

    def left_columns(place_ref, a_ref, k):
        start, stop = spans[k]
        return [
            a_ref[:, columns(flipped(place_ref, bits), start, stop - start)]
            for bits in range(devs)
        ]

    def cuts_of(k):
        size = spans[k][1] - spans[k][0]
        if k == len(groups) - 1:
            return []
        shares = SHARES
        edges = [0] + [round(size * share / 16) * 16 for share in shares]
        return list(zip(edges[:-1], edges[1:]))

    def stage_near(k):
        size = spans[k][1] - spans[k][0]
        cuts = cuts_of(k)

        def kernel(place_ref, a_ref, share_ref, *refs):
            held, near_ref, outs = refs[: devs - 1], refs[devs - 1], refs[devs:]
            left = left_columns(place_ref, a_ref, k)
            for stack_ref, (low, high) in zip(outs, cuts):
                for i in range(devs - 1):
                    stack_ref[i] = held[i][low:high, :]
            if not cuts:
                outs[0][...] = held[-1][...]
            value = jnp.dot(left[0], share_ref[...], preferred_element_type=f32)
            for bits in range(1, devs):
                value += jnp.dot(left[bits], held[bits - 1][...], preferred_element_type=f32)
            near_ref[...] = value

        near, *stacks = run(
            kernel,
            [((tokens, half), f32)]
            + [((devs - 1, high - low, half), bf16) for low, high in cuts]
            + ([] if cuts else [((size, half), bf16)]),
            activations,
            group[k]["share"],
            *group[k]["held"],
        )
        blocks = stacks if cuts else group[k]["held"][:-1] + stacks
        group[k].update(near=near, swapped=[flip(block, "region", 1) for block in blocks])

    def stage_project(k):
        final = k == len(groups) - 1
        cuts = cuts_of(k)
        count = len(cuts) or devs - 1

        def kernel(place_ref, a_ref, fresh_ref, near_ref, *refs):
            swapped, out_ref = refs[:count], refs[-1]
            left = left_columns(place_ref, a_ref, k)
            core = place_ref[2]
            near_at = pl.ds(pl.multiple_of(core * half, LANES), half)
            far_at = pl.ds(pl.multiple_of((1 - core) * half, LANES), half)
            far = jnp.dot(left[0], fresh_ref[:, far_at], preferred_element_type=f32)
            for bits in range(1, devs):
                if cuts:
                    right = jnp.concatenate([part[bits - 1] for part in swapped], axis=0)
                else:
                    right = swapped[bits - 1][...]
                far += jnp.dot(left[bits], right, preferred_element_type=f32)
            for value, at in ((near_ref[...], near_at), (far, far_at)):
                if k:
                    value = value + refs[count][:, at]
                if final:
                    value = value * (1.0 / math.sqrt(features))
                out_ref[:, at] = value.astype(out_ref.dtype)

        operands = [activations, group[k]["fresh"], group[k]["near"], *group[k]["swapped"]]
        operands += [group[k - 1]["total"]] if k else []
        (total,) = run(kernel, [((tokens, width), bf16 if final else f32)], *operands)
        group[k]["total"] = total

    results = {}

    def stage_moments(k):
        def kernel(place_ref, m_ref, v_ref, *refs):
            for part, span in zip(refs, [pl.ds(low, high - low) for low, high in spans]):
                refs[-2][span, :], refs[-1][span, :] = moments(
                    part[...], m_ref[span, :], v_ref[span, :]
                )

        results["moments"] = run(
            kernel,
            [((rows, width), f32)] * 2,
            first,
            second,
            *[p["gradient"] for p in group],
            mark=True,
        )

    def stage_velocity(k):
        def kernel(place_ref, m_ref, *refs):
            for part, span in zip(refs, [pl.ds(low, high - low) for low, high in spans]):
                refs[-1][span, :] = region_mu * m_ref[span, :] + part[...]

        results["velocity"] = run(
            kernel, [((rows, width), f32)], momentum, *[p["mean"] for p in group], late=-1, mark=True
        )

    def stage_outer(k):
        def kernel(place_ref, g_ref, m_ref, *refs):
            for part, span in zip(refs, [pl.ds(low, high - low) for low, high in spans]):
                velocity, fresh = outer(part[...], g_ref[span, :], m_ref[span, :])
                refs[-2][span, :] = velocity
                refs[-1][span, :] = fresh

        results["outer"] = run(
            kernel,
            [((rows, width), f32)] * 2,
            global_anchor,
            global_momentum,
            *[p["global_mean"] for p in group],
            mark=True,
        )

    stages = {
        "c": stage_message,
        "x": stage_own,
        "s": stage_sums,
        "b": stage_bases,
        "a": stage_adam,
        "p": stage_pair,
        "q": stage_means,
        "y": stage_relay,
        "k": stage_near,
        "j": stage_project,
        "m": stage_moments,
        "v": stage_velocity,
        "o": stage_outer,
    }
    for step in plan_of(len(pieces), len(groups)):
        stages[step[0]](int(step[1:]))

    return (
        results["moments"][0][None, None],
        results["moments"][1][None, None],
        results["velocity"][0][None],
        results["outer"][0],
        results["outer"][1],
        group[-1]["total"],
    )


def groups_of(count):
    return GROUPS if count == len(SIZES) else [[k] for k in range(count)]


def plan_of(count, groups):
    if count == len(SIZES):
        return ORDER
    steps = ["c%d" % k for k in range(count)] + ["x%d" % k for k in range(count)]
    steps += ["s%d" % k for k in range(count)] + ["b0"]
    for letter in "apq":
        steps += [letter + "%d" % k for k in range(groups)]
    steps += ["v0", "o0", "m0", "y%d" % (groups - 1)]
    for letter in "kj":
        steps += [letter + "%d" % k for k in range(groups)]
    return steps


def solution(mesh):
    devs, islands, regions = mesh.shape["dev"], mesh.shape["island"], mesh.shape["region"]
    aligned = DW % (devs * LANES) == 0
    paired = devs == 4 and islands == 4 and regions == 2 and aligned
    return jax.shard_map(
        paired_body if paired else generic_body,
        mesh=mesh,
        in_specs=(
            P(("region", "island", "dev"), None),
            P(("region", "island", "dev"), None),
            P("region", "island", "dev", None),
            P("region", "island", "dev", None),
            P("region", "island", "dev", None),
            P("region", "dev", None),
            P("region", "dev", None),
            P("dev", None),
            P("dev", None),
        ),
        out_specs=(
            P("region", "island", "dev", None),
            P("region", "island", "dev", None),
            P("region", "dev", None),
            P("dev", None),
            P("dev", None),
            P(("region", "island", "dev"), None),
        ),
        check_vma=False,
    )
```

```python
import math

import jax
import jax.numpy as jnp
from jax import lax
from jax.experimental import pallas as pl
from jax.experimental.pallas import tpu as pltpu
from jax.sharding import PartitionSpec as P

DW = 2560
LANES = 128
VMEM_BYTES = 16 * 2**20
SIZES = [2, 3]
GROUPS = [[0], [1]]
SHARES = (3 / 4, 1.0)
ORDER = ("c0", "c1", "x0", "x1", "b0", "s0", "s1", "a0", "p0", "q0", "a1", "p1", "k0", "q1", "j0", "v1", "o1", "y1", "m1", "k1", "j1")


beta_first = 0.9
beta_second = 0.999
adam_eps = 1e-08
inner_rate = 0.05
weight_decay = 0.1
region_mu = 0.9
region_rate = 0.7
global_mu = 0.9
global_rate = 0.7


def moments(gradient, adam_first, adam_second):
    first_new = beta_first * adam_first + (1.0 - beta_first) * gradient
    second_new = beta_second * adam_second + (1.0 - beta_second) * gradient * gradient
    return first_new, second_new


def adam(gradient, island_weight, adam_first, adam_second):
    first_new, second_new = moments(gradient, adam_first, adam_second)
    inner = island_weight - inner_rate * (
        first_new / (jnp.sqrt(second_new) + adam_eps) + weight_decay * island_weight
    )
    return first_new, second_new, inner


def regional(region_mean, region_anchor, region_momentum):
    region_velocity = region_mu * region_momentum + region_mean
    region_params = region_anchor - region_rate * (region_mean + region_mu * region_velocity)
    return region_velocity, region_params


def outer(global_mean, global_anchor, global_momentum):
    global_velocity = global_mu * global_momentum + global_mean
    global_new = global_anchor - global_rate * (global_mean + global_mu * global_velocity)
    return global_velocity, global_new


def generic_body(
    activations,
    cotangent,
    island_weight,
    adam_first,
    adam_second,
    region_anchor,
    region_momentum,
    global_anchor,
    global_momentum,
):
    island_tokens = activations.shape[0] * lax.axis_size("dev")
    islands = lax.axis_size("island")
    regions = lax.axis_size("region")
    summed = lax.psum_scatter(
        lax.dot_general(
            activations, cotangent, (((0,), (0,)), ((), ())), preferred_element_type=jnp.float32
        ).astype(jnp.bfloat16),
        "dev",
        scatter_dimension=0,
        tiled=True,
    ).astype(jnp.float32)
    gradient = summed * (1.0 / math.sqrt(island_tokens))
    first_new, second_new, inner = adam(gradient, island_weight, adam_first, adam_second)
    island_delta = region_anchor[:, None] - inner
    region_mean = lax.psum(island_delta, "island")[:, 0] / islands
    region_velocity, region_params = regional(region_mean, region_anchor, region_momentum)
    region_gap = global_anchor[None] - region_params
    global_mean = lax.psum(region_gap, "region")[0] / regions
    global_velocity, global_new = outer(global_mean, global_anchor, global_momentum)
    weight_full = lax.all_gather(global_new.astype(jnp.bfloat16), "dev", axis=0, tiled=True)
    projected = jnp.dot(activations, weight_full, preferred_element_type=jnp.float32)
    next_keys = (projected * (1.0 / math.sqrt(activations.shape[1]))).astype(jnp.bfloat16)
    return (first_new, second_new, region_velocity, global_velocity, global_new, next_keys)


def flip(array, axis, bits):
    return lax.ppermute(array, axis, [(i, i ^ bits) for i in range(lax.axis_size(axis))])


def chunks_of(rows):
    units = rows // LANES
    sizes = SIZES if sum(SIZES) == units else [1] * units
    edges = [0]
    for size in sizes:
        edges.append(edges[-1] + size * LANES)
    return list(zip(edges[:-1], edges[1:]))


def local_kernel(kernel, out_shapes, place, *operands, order):
    def with_order(place_ref, *refs):
        kernel(place_ref, *refs[len(order) :])

    whole = pl.BlockSpec(memory_space=pltpu.VMEM)
    return pl.pallas_call(
        with_order,
        out_shape=[jax.ShapeDtypeStruct(shape, dtype) for shape, dtype in out_shapes],
        in_specs=[pl.BlockSpec(memory_space=pltpu.SMEM)]
        + [pl.BlockSpec(memory_space=pl.ANY)] * len(order)
        + [whole] * len(operands),
        out_specs=[whole] * len(out_shapes),
        compiler_params=pltpu.CompilerParams(vmem_limit_bytes=VMEM_BYTES),
        cost_estimate=pl.CostEstimate(flops=1, bytes_accessed=1, transcendentals=0),
    )(place, *order, *operands)


def flipped(place, bits):
    return 2 * (place[1] ^ (bits >> 1)) + (place[0] ^ (bits & 1))


def product(left, right):
    return lax.dot_general(
        left, right, (((0,), (0,)), ((), ())), preferred_element_type=jnp.float32
    )


def paired_body(
    activations,
    cotangent,
    island_weight,
    adam_first,
    adam_second,
    region_anchor,
    region_momentum,
    global_anchor,
    global_momentum,
):
    f32, bf16 = jnp.float32, jnp.bfloat16
    devs = lax.axis_size("dev")
    islands = lax.axis_size("island")
    regions = lax.axis_size("region")
    tokens, features = activations.shape
    width = cotangent.shape[1]
    half = width // regions
    rows = features // devs
    scale = 1.0 / math.sqrt(tokens * devs)
    me = lax.axis_index("dev")
    place = jnp.stack([me & 1, me >> 1, lax.axis_index("region")]).astype(jnp.int32)
    weight, first, second = island_weight[0, 0], adam_first[0, 0], adam_second[0, 0]
    anchor, momentum = region_anchor[0], region_momentum[0]
    pieces = chunks_of(rows)
    groups = groups_of(len(pieces))
    spans = [(pieces[members[0]][0], pieces[members[-1]][1]) for members in groups]
    group = [{} for _ in groups]
    bases = []
    token = [place]
    state = [{} for _ in pieces]

    def run(kernel, out_shapes, *operands, mark=False, after=()):
        order = [token[0], *after]
        if mark:

            def marked(place_ref, *refs):
                kernel(place_ref, *refs[:-1])
                refs[-1][...] = jnp.zeros_like(refs[-1])

            small = (8, LANES)
            *outs, token[0] = local_kernel(
                marked, [*out_shapes, (small, f32)], place, *operands, order=order
            )
            return outs
        outs = local_kernel(kernel, out_shapes, place, *operands, order=order)
        token[0] = outs[0]
        return outs

    def columns(shard, start, size):
        return pl.ds(pl.multiple_of(shard * rows + start, LANES), size)

    def stage_message(k):
        start, stop = pieces[k]
        size = stop - start
        extra = width if k == 0 else 0

        def kernel(place_ref, *refs):
            a_ref, out_ref = refs[0], refs[-1]
            for i, bits in enumerate((1, 3)):
                at = columns(flipped(place_ref, bits), start, size)
                out_ref[:, i * size : (i + 1) * size] = a_ref[:, at]
            if extra:
                out_ref[:, 2 * size :] = refs[1][...]

        operands = (activations, cotangent) if extra else (activations,)
        (message,) = run(kernel, [((tokens, 2 * size + extra), bf16)], *operands)
        state[k]["raw"] = flip(message, "dev", 1)

    def stage_own(k):
        start, stop = pieces[k]
        size = stop - start

        def kernel(place_ref, a_ref, c_ref, kept_ref, away_ref):
            for bits, ref in ((0, kept_ref), (2, away_ref)):
                at = columns(flipped(place_ref, bits), start, size)
                ref[...] = product(a_ref[:, at], c_ref[...])

        state[k]["own"] = run(kernel, [((size, width), f32)] * 2, activations, cotangent)

    def partner_cotangent(first_ref):
        return first_ref[:, first_ref.shape[1] - width :]

    def stage_sums(k):
        start, stop = pieces[k]
        size = stop - start

        def kernel(place_ref, own_ref, raw_ref, *refs):
            first_ref = refs[0] if k else raw_ref
            out_ref = refs[-1]
            part = product(raw_ref[:, size : 2 * size], partner_cotangent(first_ref))
            out_ref[...] = (own_ref[...] + part).astype(bf16)

        operands = [state[k]["own"][1], state[k]["raw"]] + ([state[0]["raw"]] if k else [])
        (sums,) = run(kernel, [((size, width), bf16)], *operands)
        state[k]["sum"] = flip(sums, "dev", 2)

    def stage_bases(k):
        def kernel(place_ref, w_ref, r_ref, rm_ref, g_ref, gm_ref, delta_ref, gap_ref, new_ref):
            delta_ref[...] = r_ref[...] - (1.0 - inner_rate * weight_decay) * w_ref[...]
            _, params = regional(0.0, r_ref[...], rm_ref[...])
            gap_ref[...] = g_ref[...] - params
            _, new_ref[...] = outer(0.0, g_ref[...], gm_ref[...])

        bases[:] = run(
            kernel,
            [((rows, width), f32)] * 3,
            weight,
            anchor,
            momentum,
            global_anchor,
            global_momentum,
        )
        bases.append(flip(bases[1], "region", 1))

    def stage_adam(g):
        members = groups[g]
        start, stop = spans[g]
        size = stop - start

        def kernel(place_ref, m_ref, v_ref, base_ref, first_ref, *refs):
            delta_ref, gradient_ref = refs[-2:]
            for i, k in enumerate(members):
                low, high = pieces[k]
                count = high - low
                own_ref, raw_ref, sum_ref = refs[3 * i : 3 * i + 3]
                part = product(raw_ref[:, :count], partner_cotangent(first_ref))
                gradient = (own_ref[...] + part + sum_ref[...].astype(f32)) * scale
                span = pl.ds(low, count)
                first_new, second_new = moments(gradient, m_ref[span, :], v_ref[span, :])
                step = inner_rate * (first_new / (jnp.sqrt(second_new) + adam_eps))
                here = pl.ds(low - start, count)
                delta_ref[here, :] = (base_ref[span, :] + step).astype(bf16)
                gradient_ref[here, :] = gradient

        operands = [first, second, bases[0], state[0]["raw"]]
        for k in members:
            operands += [state[k]["own"][0], state[k]["raw"], state[k]["sum"]]
        delta, gradient = run(kernel, [((size, width), bf16), ((size, width), f32)], *operands)
        group[g].update(delta=delta, gradient=gradient, pair=halves(delta, (1, 2)))

    def halves(array, bits):
        middle = array.shape[0] // 2
        return [flip(array[:middle], "island", bits[0]), flip(array[middle:], "island", bits[1])]

    def summed(mine_ref, upper_ref, lower_ref):
        other = jnp.concatenate([upper_ref[...], lower_ref[...]], axis=0)
        return mine_ref[...].astype(f32) + other.astype(f32)

    def stage_pair(k):
        def kernel(place_ref, mine_ref, upper_ref, lower_ref, out_ref):
            out_ref[...] = summed(mine_ref, upper_ref, lower_ref).astype(bf16)

        (pair,) = run(
            kernel, [(group[k]["delta"].shape, bf16)], group[k]["delta"], *group[k]["pair"]
        )
        rest = halves(pair, (2, 1))
        group[k].update(mine=pair, rest=rest, mine2=flip(pair, "region", 1))
        group[k]["rest2"] = [flip(part, "region", 1) for part in rest]

    def stage_means(k):
        start, stop = spans[k]
        size = stop - start
        span = pl.ds(start, size)

        def kernel(place_ref, mine, up, low, mine2, up2, low2, base, base2, new, *outs):
            fresh_ref, share_ref, mean_ref, global_ref = outs
            gain = region_rate * (1.0 + region_mu)
            mean = summed(mine, up, low) / islands
            mean_ref[...] = mean
            gap = base[span, :] + gain * mean
            gap += base2[span, :] + gain * (summed(mine2, up2, low2) / islands)
            mean = gap / regions
            global_ref[...] = mean
            fresh = new[span, :] - global_rate * (1.0 + global_mu) * mean
            fresh_ref[...] = fresh.astype(bf16)
            at = pl.ds(pl.multiple_of(place_ref[2] * half, LANES), half)
            share_ref[...] = fresh_ref[:, at]

        this = group[k]
        fresh, share, mean, global_mean = run(
            kernel,
            [((size, width), bf16), ((size, half), bf16)] + [((size, width), f32)] * 2,
            this["mine"],
            *this["rest"],
            this["mine2"],
            *this["rest2"],
            bases[1],
            bases[3],
            bases[2],
            after=[group[k - 1]["swapped"][0]] if k and "swapped" in group[k - 1] else [],
        )
        held = [flip(share, "dev", 1), flip(share, "dev", 2)]
        if k < len(groups) - 1:
            held.append(flip(share, "dev", 3))
        this.update(mean=mean, fresh=fresh, share=share, global_mean=global_mean, held=held)

    def stage_relay(k):
        def kernel(place_ref, block_ref, out_ref):
            out_ref[...] = block_ref[...]

        block = group[k]["held"][1]
        (block,) = run(kernel, [(block.shape, bf16)], block)
        group[k]["held"].append(flip(block, "dev", 1))

    def left_columns(place_ref, a_ref, k):
        start, stop = spans[k]
        return [
            a_ref[:, columns(flipped(place_ref, bits), start, stop - start)]
            for bits in range(devs)
        ]

    def cuts_of(k):
        size = spans[k][1] - spans[k][0]
        if k == len(groups) - 1:
            return []
        shares = SHARES
        edges = [0] + [round(size * share / 16) * 16 for share in shares]
        return list(zip(edges[:-1], edges[1:]))

    def stage_near(k):
        size = spans[k][1] - spans[k][0]
        cuts = cuts_of(k)

        def kernel(place_ref, a_ref, share_ref, *refs):
            held, near_ref, outs = refs[: devs - 1], refs[devs - 1], refs[devs:]
            left = left_columns(place_ref, a_ref, k)
            for stack_ref, (low, high) in zip(outs, cuts):
                for i in range(devs - 1):
                    stack_ref[i] = held[i][low:high, :]
            if not cuts:
                outs[0][...] = held[-1][...]
            value = jnp.dot(left[0], share_ref[...], preferred_element_type=f32)
            for bits in range(1, devs):
                value += jnp.dot(left[bits], held[bits - 1][...], preferred_element_type=f32)
            near_ref[...] = value

        near, *stacks = run(
            kernel,
            [((tokens, half), f32)]
            + [((devs - 1, high - low, half), bf16) for low, high in cuts]
            + ([] if cuts else [((size, half), bf16)]),
            activations,
            group[k]["share"],
            *group[k]["held"],
        )
        blocks = stacks if cuts else group[k]["held"][:-1] + stacks
        group[k].update(near=near, swapped=[flip(block, "region", 1) for block in blocks])

    def stage_project(k):
        final = k == len(groups) - 1
        cuts = cuts_of(k)
        count = len(cuts) or devs - 1

        def kernel(place_ref, a_ref, fresh_ref, near_ref, *refs):
            swapped, out_ref = refs[:count], refs[-1]
            left = left_columns(place_ref, a_ref, k)
            core = place_ref[2]
            near_at = pl.ds(pl.multiple_of(core * half, LANES), half)
            far_at = pl.ds(pl.multiple_of((1 - core) * half, LANES), half)
            far = jnp.dot(left[0], fresh_ref[:, far_at], preferred_element_type=f32)
            for bits in range(1, devs):
                if cuts:
                    right = jnp.concatenate([part[bits - 1] for part in swapped], axis=0)
                else:
                    right = swapped[bits - 1][...]
                far += jnp.dot(left[bits], right, preferred_element_type=f32)
            for value, at in ((near_ref[...], near_at), (far, far_at)):
                if k:
                    value = value + refs[count][:, at]
                if final:
                    value = value * (1.0 / math.sqrt(features))
                out_ref[:, at] = value.astype(out_ref.dtype)

        operands = [activations, group[k]["fresh"], group[k]["near"], *group[k]["swapped"]]
        operands += [group[k - 1]["total"]] if k else []
        (total,) = run(kernel, [((tokens, width), bf16 if final else f32)], *operands)
        group[k]["total"] = total

    results = {}

    def stage_moments(k):
        def kernel(place_ref, m_ref, v_ref, *refs):
            for part, span in zip(refs, [pl.ds(low, high - low) for low, high in spans]):
                refs[-2][span, :], refs[-1][span, :] = moments(
                    part[...], m_ref[span, :], v_ref[span, :]
                )

        results["moments"] = run(
            kernel,
            [((rows, width), f32)] * 2,
            first,
            second,
            *[p["gradient"] for p in group],
            mark=True,
        )

    def stage_velocity(k):
        def kernel(place_ref, m_ref, *refs):
            for part, span in zip(refs, [pl.ds(low, high - low) for low, high in spans]):
                refs[-1][span, :] = region_mu * m_ref[span, :] + part[...]

        results["velocity"] = run(
            kernel, [((rows, width), f32)], momentum, *[p["mean"] for p in group], mark=True
        )

    def stage_outer(k):
        def kernel(place_ref, g_ref, m_ref, *refs):
            for part, span in zip(refs, [pl.ds(low, high - low) for low, high in spans]):
                velocity, fresh = outer(part[...], g_ref[span, :], m_ref[span, :])
                refs[-2][span, :] = velocity
                refs[-1][span, :] = fresh

        results["outer"] = run(
            kernel,
            [((rows, width), f32)] * 2,
            global_anchor,
            global_momentum,
            *[p["global_mean"] for p in group],
            mark=True,
        )

    stages = {
        "c": stage_message,
        "x": stage_own,
        "s": stage_sums,
        "b": stage_bases,
        "a": stage_adam,
        "p": stage_pair,
        "q": stage_means,
        "y": stage_relay,
        "k": stage_near,
        "j": stage_project,
        "m": stage_moments,
        "v": stage_velocity,
        "o": stage_outer,
    }
    for step in plan_of(len(pieces), len(groups)):
        stages[step[0]](int(step[1:]))

    return (
        results["moments"][0][None, None],
        results["moments"][1][None, None],
        results["velocity"][0][None],
        results["outer"][0],
        results["outer"][1],
        group[-1]["total"],
    )


def groups_of(count):
    return GROUPS if count == len(SIZES) else [[k] for k in range(count)]


def plan_of(count, groups):
    if count == len(SIZES):
        return ORDER
    steps = ["c%d" % k for k in range(count)] + ["x%d" % k for k in range(count)]
    steps += ["s%d" % k for k in range(count)] + ["b0"]
    for letter in "apq":
        steps += [letter + "%d" % k for k in range(groups)]
    steps += ["v0", "o0", "m0", "y%d" % (groups - 1)]
    for letter in "kj":
        steps += [letter + "%d" % k for k in range(groups)]
    return steps


def solution(mesh):
    devs, islands, regions = mesh.shape["dev"], mesh.shape["island"], mesh.shape["region"]
    aligned = DW % (devs * LANES) == 0
    paired = devs == 4 and islands == 4 and regions == 2 and aligned
    return jax.shard_map(
        paired_body if paired else generic_body,
        mesh=mesh,
        in_specs=(
            P(("region", "island", "dev"), None),
            P(("region", "island", "dev"), None),
            P("region", "island", "dev", None),
            P("region", "island", "dev", None),
            P("region", "island", "dev", None),
            P("region", "dev", None),
            P("region", "dev", None),
            P("dev", None),
            P("dev", None),
        ),
        out_specs=(
            P("region", "island", "dev", None),
            P("region", "island", "dev", None),
            P("region", "dev", None),
            P("dev", None),
            P("dev", None),
            P(("region", "island", "dev"), None),
        ),
        check_vma=False,
    )
```

```python
import math

import jax
import jax.numpy as jnp
from jax import lax
from jax.experimental import pallas as pl
from jax.experimental.pallas import tpu as pltpu
from jax.sharding import PartitionSpec as P

DW = 2560
LANES = 128
VMEM_BYTES = 16 * 2**20
SIZES = [2, 3]
GROUPS = [[0], [1]]
SHARES = (3 / 4, 1.0)
ORDER = ("c0", "c1", "x0", "x1", "b0", "s0", "s1", "a0", "p0", "q0", "a1", "p1", "k0", "q1", "j0", "v1", "o1", "y1", "m1", "k1", "j1")


beta_first = 0.9
beta_second = 0.999
adam_eps = 1e-08
inner_rate = 0.05
weight_decay = 0.1
region_mu = 0.9
region_rate = 0.7
global_mu = 0.9
global_rate = 0.7


def moments(gradient, adam_first, adam_second):
    first_new = beta_first * adam_first + (1.0 - beta_first) * gradient
    second_new = beta_second * adam_second + (1.0 - beta_second) * gradient * gradient
    return first_new, second_new


def adam(gradient, island_weight, adam_first, adam_second):
    first_new, second_new = moments(gradient, adam_first, adam_second)
    inner = island_weight - inner_rate * (
        first_new / (jnp.sqrt(second_new) + adam_eps) + weight_decay * island_weight
    )
    return first_new, second_new, inner


def regional(region_mean, region_anchor, region_momentum):
    region_velocity = region_mu * region_momentum + region_mean
    region_params = region_anchor - region_rate * (region_mean + region_mu * region_velocity)
    return region_velocity, region_params


def outer(global_mean, global_anchor, global_momentum):
    global_velocity = global_mu * global_momentum + global_mean
    global_new = global_anchor - global_rate * (global_mean + global_mu * global_velocity)
    return global_velocity, global_new


def generic_body(
    activations,
    cotangent,
    island_weight,
    adam_first,
    adam_second,
    region_anchor,
    region_momentum,
    global_anchor,
    global_momentum,
):
    island_tokens = activations.shape[0] * lax.axis_size("dev")
    islands = lax.axis_size("island")
    regions = lax.axis_size("region")
    summed = lax.psum_scatter(
        lax.dot_general(
            activations, cotangent, (((0,), (0,)), ((), ())), preferred_element_type=jnp.float32
        ).astype(jnp.bfloat16),
        "dev",
        scatter_dimension=0,
        tiled=True,
    ).astype(jnp.float32)
    gradient = summed * (1.0 / math.sqrt(island_tokens))
    first_new, second_new, inner = adam(gradient, island_weight, adam_first, adam_second)
    island_delta = region_anchor[:, None] - inner
    region_mean = lax.psum(island_delta, "island")[:, 0] / islands
    region_velocity, region_params = regional(region_mean, region_anchor, region_momentum)
    region_gap = global_anchor[None] - region_params
    global_mean = lax.psum(region_gap, "region")[0] / regions
    global_velocity, global_new = outer(global_mean, global_anchor, global_momentum)
    weight_full = lax.all_gather(global_new.astype(jnp.bfloat16), "dev", axis=0, tiled=True)
    projected = jnp.dot(activations, weight_full, preferred_element_type=jnp.float32)
    next_keys = (projected * (1.0 / math.sqrt(activations.shape[1]))).astype(jnp.bfloat16)
    return (first_new, second_new, region_velocity, global_velocity, global_new, next_keys)


def flip(array, axis, bits):
    return lax.ppermute(array, axis, [(i, i ^ bits) for i in range(lax.axis_size(axis))])


def chunks_of(rows):
    units = rows // LANES
    sizes = SIZES if sum(SIZES) == units else [1] * units
    edges = [0]
    for size in sizes:
        edges.append(edges[-1] + size * LANES)
    return list(zip(edges[:-1], edges[1:]))


def local_kernel(kernel, out_shapes, place, *operands, order):
    def with_order(place_ref, *refs):
        kernel(place_ref, *refs[len(order) :])

    whole = pl.BlockSpec(memory_space=pltpu.VMEM)
    return pl.pallas_call(
        with_order,
        out_shape=[jax.ShapeDtypeStruct(shape, dtype) for shape, dtype in out_shapes],
        in_specs=[pl.BlockSpec(memory_space=pltpu.SMEM)]
        + [pl.BlockSpec(memory_space=pl.ANY)] * len(order)
        + [whole] * len(operands),
        out_specs=[whole] * len(out_shapes),
        compiler_params=pltpu.CompilerParams(vmem_limit_bytes=VMEM_BYTES),
        cost_estimate=pl.CostEstimate(flops=1, bytes_accessed=1, transcendentals=0),
    )(place, *order, *operands)


def flipped(place, bits):
    return 2 * (place[1] ^ (bits >> 1)) + (place[0] ^ (bits & 1))


def product(left, right):
    return lax.dot_general(
        left, right, (((0,), (0,)), ((), ())), preferred_element_type=jnp.float32
    )


def paired_body(
    activations,
    cotangent,
    island_weight,
    adam_first,
    adam_second,
    region_anchor,
    region_momentum,
    global_anchor,
    global_momentum,
):
    f32, bf16 = jnp.float32, jnp.bfloat16
    devs = lax.axis_size("dev")
    islands = lax.axis_size("island")
    regions = lax.axis_size("region")
    tokens, features = activations.shape
    width = cotangent.shape[1]
    half = width // regions
    rows = features // devs
    scale = 1.0 / math.sqrt(tokens * devs)
    me = lax.axis_index("dev")
    place = jnp.stack([me & 1, me >> 1, lax.axis_index("region")]).astype(jnp.int32)
    weight, first, second = island_weight[0, 0], adam_first[0, 0], adam_second[0, 0]
    anchor, momentum = region_anchor[0], region_momentum[0]
    pieces = chunks_of(rows)
    groups = groups_of(len(pieces))
    spans = [(pieces[members[0]][0], pieces[members[-1]][1]) for members in groups]
    group = [{} for _ in groups]
    bases = []
    token = [place]
    state = [{} for _ in pieces]

    def run(kernel, out_shapes, *operands, mark=False, after=()):
        order = [token[0], *after]
        if mark:

            def marked(place_ref, *refs):
                kernel(place_ref, *refs[:-1])
                refs[-1][...] = jnp.zeros_like(refs[-1])

            small = (8, LANES)
            *outs, token[0] = local_kernel(
                marked, [*out_shapes, (small, f32)], place, *operands, order=order
            )
            return outs
        outs = local_kernel(kernel, out_shapes, place, *operands, order=order)
        token[0] = outs[0]
        return outs

    def columns(shard, start, size):
        return pl.ds(pl.multiple_of(shard * rows + start, LANES), size)

    def stage_message(k):
        start, stop = pieces[k]
        size = stop - start

        def kernel(place_ref, a_ref, out_ref):
            for i, bits in enumerate((1, 3)):
                at = columns(flipped(place_ref, bits), start, size)
                out_ref[:, i * size : (i + 1) * size] = a_ref[:, at]

        if k:
            (message,) = run(kernel, [((tokens, 2 * size), bf16)], activations)
        else:
            at = [activations[:, i * rows + start : i * rows + stop] for i in range(devs)]
            lower, upper = [
                jnp.where(place[0] == 0, at[2 * i + 1], at[2 * i]) for i in range(devs // 2)
            ]
            kept = jnp.where(place[1] == 0, lower, upper)
            sent = jnp.where(place[1] == 0, upper, lower)
            message = jnp.concatenate([kept, sent, cotangent], axis=1)
            token[0] = message
        state[k]["raw"] = flip(message, "dev", 1)

    def stage_own(k):
        start, stop = pieces[k]
        size = stop - start

        def kernel(place_ref, a_ref, c_ref, kept_ref, away_ref):
            for bits, ref in ((0, kept_ref), (2, away_ref)):
                at = columns(flipped(place_ref, bits), start, size)
                ref[...] = product(a_ref[:, at], c_ref[...])

        state[k]["own"] = run(kernel, [((size, width), f32)] * 2, activations, cotangent)

    def partner_cotangent(first_ref):
        return first_ref[:, first_ref.shape[1] - width :]

    def stage_sums(k):
        start, stop = pieces[k]
        size = stop - start

        def kernel(place_ref, own_ref, raw_ref, *refs):
            first_ref = refs[0] if k else raw_ref
            out_ref = refs[-1]
            part = product(raw_ref[:, size : 2 * size], partner_cotangent(first_ref))
            out_ref[...] = (own_ref[...] + part).astype(bf16)

        operands = [state[k]["own"][1], state[k]["raw"]] + ([state[0]["raw"]] if k else [])
        (sums,) = run(kernel, [((size, width), bf16)], *operands)
        state[k]["sum"] = flip(sums, "dev", 2)

    def stage_bases(k):
        def kernel(place_ref, w_ref, r_ref, rm_ref, g_ref, gm_ref, delta_ref, gap_ref, new_ref):
            delta_ref[...] = r_ref[...] - (1.0 - inner_rate * weight_decay) * w_ref[...]
            _, params = regional(0.0, r_ref[...], rm_ref[...])
            gap_ref[...] = g_ref[...] - params
            _, new_ref[...] = outer(0.0, g_ref[...], gm_ref[...])

        bases[:] = run(
            kernel,
            [((rows, width), f32)] * 3,
            weight,
            anchor,
            momentum,
            global_anchor,
            global_momentum,
        )
        bases.append(flip(bases[1], "region", 1))

    def stage_adam(g):
        members = groups[g]
        start, stop = spans[g]
        size = stop - start

        def kernel(place_ref, m_ref, v_ref, base_ref, first_ref, *refs):
            delta_ref, gradient_ref = refs[-2:]
            for i, k in enumerate(members):
                low, high = pieces[k]
                count = high - low
                own_ref, raw_ref, sum_ref = refs[3 * i : 3 * i + 3]
                part = product(raw_ref[:, :count], partner_cotangent(first_ref))
                gradient = (own_ref[...] + part + sum_ref[...].astype(f32)) * scale
                span = pl.ds(low, count)
                first_new, second_new = moments(gradient, m_ref[span, :], v_ref[span, :])
                step = inner_rate * (first_new / (jnp.sqrt(second_new) + adam_eps))
                here = pl.ds(low - start, count)
                delta_ref[here, :] = (base_ref[span, :] + step).astype(bf16)
                gradient_ref[here, :] = gradient

        operands = [first, second, bases[0], state[0]["raw"]]
        for k in members:
            operands += [state[k]["own"][0], state[k]["raw"], state[k]["sum"]]
        delta, gradient = run(kernel, [((size, width), bf16), ((size, width), f32)], *operands)
        group[g].update(delta=delta, gradient=gradient, pair=halves(delta, (1, 2)))

    def halves(array, bits):
        middle = array.shape[0] // 2
        return [flip(array[:middle], "island", bits[0]), flip(array[middle:], "island", bits[1])]

    def summed(mine_ref, upper_ref, lower_ref):
        other = jnp.concatenate([upper_ref[...], lower_ref[...]], axis=0)
        return mine_ref[...].astype(f32) + other.astype(f32)

    def stage_pair(k):
        def kernel(place_ref, mine_ref, upper_ref, lower_ref, out_ref):
            out_ref[...] = summed(mine_ref, upper_ref, lower_ref).astype(bf16)

        (pair,) = run(
            kernel, [(group[k]["delta"].shape, bf16)], group[k]["delta"], *group[k]["pair"]
        )
        rest = halves(pair, (2, 1))
        group[k].update(mine=pair, rest=rest, mine2=flip(pair, "region", 1))
        group[k]["rest2"] = [flip(part, "region", 1) for part in rest]

    def stage_means(k):
        start, stop = spans[k]
        size = stop - start
        span = pl.ds(start, size)

        def kernel(place_ref, mine, up, low, mine2, up2, low2, base, base2, new, *outs):
            fresh_ref, share_ref, mean_ref, global_ref = outs
            gain = region_rate * (1.0 + region_mu)
            mean = summed(mine, up, low) / islands
            mean_ref[...] = mean
            gap = base[span, :] + gain * mean
            gap += base2[span, :] + gain * (summed(mine2, up2, low2) / islands)
            mean = gap / regions
            global_ref[...] = mean
            fresh = new[span, :] - global_rate * (1.0 + global_mu) * mean
            fresh_ref[...] = fresh.astype(bf16)
            at = pl.ds(pl.multiple_of(place_ref[2] * half, LANES), half)
            share_ref[...] = fresh_ref[:, at]

        this = group[k]
        fresh, share, mean, global_mean = run(
            kernel,
            [((size, width), bf16), ((size, half), bf16)] + [((size, width), f32)] * 2,
            this["mine"],
            *this["rest"],
            this["mine2"],
            *this["rest2"],
            bases[1],
            bases[3],
            bases[2],
            after=[group[k - 1]["swapped"][0]] if k and "swapped" in group[k - 1] else [],
        )
        held = [flip(share, "dev", 1), flip(share, "dev", 2)]
        if k < len(groups) - 1:
            held.append(flip(share, "dev", 3))
        this.update(mean=mean, fresh=fresh, share=share, global_mean=global_mean, held=held)

    def stage_relay(k):
        def kernel(place_ref, block_ref, out_ref):
            out_ref[...] = block_ref[...]

        block = group[k]["held"][1]
        (block,) = run(kernel, [(block.shape, bf16)], block)
        group[k]["held"].append(flip(block, "dev", 1))

    def left_columns(place_ref, a_ref, k):
        start, stop = spans[k]
        return [
            a_ref[:, columns(flipped(place_ref, bits), start, stop - start)]
            for bits in range(devs)
        ]

    def cuts_of(k):
        size = spans[k][1] - spans[k][0]
        if k == len(groups) - 1:
            return []
        shares = SHARES
        edges = [0] + [round(size * share / 16) * 16 for share in shares]
        return list(zip(edges[:-1], edges[1:]))

    def stage_near(k):
        size = spans[k][1] - spans[k][0]
        cuts = cuts_of(k)

        def kernel(place_ref, a_ref, share_ref, *refs):
            held, near_ref, outs = refs[: devs - 1], refs[devs - 1], refs[devs:]
            left = left_columns(place_ref, a_ref, k)
            for stack_ref, (low, high) in zip(outs, cuts):
                for i in range(devs - 1):
                    stack_ref[i] = held[i][low:high, :]
            if not cuts:
                outs[0][...] = held[-1][...]
            value = jnp.dot(left[0], share_ref[...], preferred_element_type=f32)
            for bits in range(1, devs):
                value += jnp.dot(left[bits], held[bits - 1][...], preferred_element_type=f32)
            near_ref[...] = value

        near, *stacks = run(
            kernel,
            [((tokens, half), f32)]
            + [((devs - 1, high - low, half), bf16) for low, high in cuts]
            + ([] if cuts else [((size, half), bf16)]),
            activations,
            group[k]["share"],
            *group[k]["held"],
        )
        blocks = stacks if cuts else group[k]["held"][:-1] + stacks
        group[k].update(near=near, swapped=[flip(block, "region", 1) for block in blocks])

    def stage_project(k):
        final = k == len(groups) - 1
        cuts = cuts_of(k)
        count = len(cuts) or devs - 1

        def kernel(place_ref, a_ref, fresh_ref, near_ref, *refs):
            swapped, out_ref = refs[:count], refs[-1]
            left = left_columns(place_ref, a_ref, k)
            core = place_ref[2]
            near_at = pl.ds(pl.multiple_of(core * half, LANES), half)
            far_at = pl.ds(pl.multiple_of((1 - core) * half, LANES), half)
            far = jnp.dot(left[0], fresh_ref[:, far_at], preferred_element_type=f32)
            for bits in range(1, devs):
                if cuts:
                    right = jnp.concatenate([part[bits - 1] for part in swapped], axis=0)
                else:
                    right = swapped[bits - 1][...]
                far += jnp.dot(left[bits], right, preferred_element_type=f32)
            for value, at in ((near_ref[...], near_at), (far, far_at)):
                if k:
                    value = value + refs[count][:, at]
                if final:
                    value = value * (1.0 / math.sqrt(features))
                out_ref[:, at] = value.astype(out_ref.dtype)

        operands = [activations, group[k]["fresh"], group[k]["near"], *group[k]["swapped"]]
        operands += [group[k - 1]["total"]] if k else []
        (total,) = run(kernel, [((tokens, width), bf16 if final else f32)], *operands)
        group[k]["total"] = total

    results = {}

    def stage_moments(k):
        def kernel(place_ref, m_ref, v_ref, *refs):
            for part, span in zip(refs, [pl.ds(low, high - low) for low, high in spans]):
                refs[-2][span, :], refs[-1][span, :] = moments(
                    part[...], m_ref[span, :], v_ref[span, :]
                )

        results["moments"] = run(
            kernel,
            [((rows, width), f32)] * 2,
            first,
            second,
            *[p["gradient"] for p in group],
            mark=True,
        )

    def stage_velocity(k):
        def kernel(place_ref, m_ref, *refs):
            for part, span in zip(refs, [pl.ds(low, high - low) for low, high in spans]):
                refs[-1][span, :] = region_mu * m_ref[span, :] + part[...]

        results["velocity"] = run(
            kernel, [((rows, width), f32)], momentum, *[p["mean"] for p in group], mark=True
        )

    def stage_outer(k):
        def kernel(place_ref, g_ref, m_ref, *refs):
            for part, span in zip(refs, [pl.ds(low, high - low) for low, high in spans]):
                velocity, fresh = outer(part[...], g_ref[span, :], m_ref[span, :])
                refs[-2][span, :] = velocity
                refs[-1][span, :] = fresh

        results["outer"] = run(
            kernel,
            [((rows, width), f32)] * 2,
            global_anchor,
            global_momentum,
            *[p["global_mean"] for p in group],
            mark=True,
        )

    stages = {
        "c": stage_message,
        "x": stage_own,
        "s": stage_sums,
        "b": stage_bases,
        "a": stage_adam,
        "p": stage_pair,
        "q": stage_means,
        "y": stage_relay,
        "k": stage_near,
        "j": stage_project,
        "m": stage_moments,
        "v": stage_velocity,
        "o": stage_outer,
    }
    for step in plan_of(len(pieces), len(groups)):
        stages[step[0]](int(step[1:]))

    return (
        results["moments"][0][None, None],
        results["moments"][1][None, None],
        results["velocity"][0][None],
        results["outer"][0],
        results["outer"][1],
        group[-1]["total"],
    )


def groups_of(count):
    return GROUPS if count == len(SIZES) else [[k] for k in range(count)]


def plan_of(count, groups):
    if count == len(SIZES):
        return ORDER
    steps = ["c%d" % k for k in range(count)] + ["x%d" % k for k in range(count)]
    steps += ["s%d" % k for k in range(count)] + ["b0"]
    for letter in "apq":
        steps += [letter + "%d" % k for k in range(groups)]
    steps += ["v0", "o0", "m0", "y%d" % (groups - 1)]
    for letter in "kj":
        steps += [letter + "%d" % k for k in range(groups)]
    return steps


def solution(mesh):
    devs, islands, regions = mesh.shape["dev"], mesh.shape["island"], mesh.shape["region"]
    aligned = DW % (devs * LANES) == 0
    paired = devs == 4 and islands == 4 and regions == 2 and aligned
    return jax.shard_map(
        paired_body if paired else generic_body,
        mesh=mesh,
        in_specs=(
            P(("region", "island", "dev"), None),
            P(("region", "island", "dev"), None),
            P("region", "island", "dev", None),
            P("region", "island", "dev", None),
            P("region", "island", "dev", None),
            P("region", "dev", None),
            P("region", "dev", None),
            P("dev", None),
            P("dev", None),
        ),
        out_specs=(
            P("region", "island", "dev", None),
            P("region", "island", "dev", None),
            P("region", "dev", None),
            P("dev", None),
            P("dev", None),
            P(("region", "island", "dev"), None),
        ),
        check_vma=False,
    )
```
